32 devices in a mesh: groups: 2 (over x), dp: 4 (over y, core), layer: 4 (over z).
Axes of the slice: x: 2, y: 2, z: 4, core: 2. Of those that a mesh axis runs over, the one named last changes fastest.
Arguments:
- activations: bfloat16 [4, 4096, 8192], P('layer', ('groups', 'dp')), parts along dimension 1, may hold values from -6 to 6
- gradients: bfloat16 [4, 4096, 4096], P('layer', ('groups', 'dp')), parts along dimension 1, may hold values from -6 to 6
- left_factors: bfloat16 [4, 512, 8192], P('layer', ('groups', 'dp')), parts along dimension 1, may hold values from -0.0625 to 0.0625
- right_factors: bfloat16 [4, 512, 4096], P('layer', ('groups', 'dp')), parts along dimension 1, may hold values from -0.09375 to 0.09375
- lengths: int32 [32], P(('groups', 'dp')), parts along dimension 0, may hold values from 1 to 256, as said below
- segment_ids: int32 [4096], P(('groups', 'dp')), parts along dimension 0, may hold values from 0 to 4, as said below
Outputs:
- scores: float32 [32, 8], P(('groups', 'dp'), 'layer'), parts along dimension 0
The draws below stay inside these ranges and needn't reach their ends.
There are 2 independent parts, one for each index of `groups`. The reference program is written for one: setup_inputs(seed, part) draws one part's arguments, and reference() takes and returns one part's arrays. A program takes and returns all parts, laid end to end along the dimension named above; each array names one. Nothing has to cross between parts.
Inputs may be any that keep to these rules, and one draw needn't show every extreme that they name: Within each dp shard the 4 lengths add up to less than 512, and exactly one of them is 256. `segment_ids`: within each dp shard of 512 slots the ids never fall, id g fills exactly lengths of that shard's sequence g, and the last slots, at least one, hold 4 (padding).
All inputs are finite; a program needn't handle non-finite values.
Results may differ from the reference program's by a relative error of at most 0.0003.
Values may be sent and summed in bfloat16 or wider, within the bound.
A program may use at most 128 MiB of HBM per device.

```python
import jax
import jax.numpy as jnp
from jax import lax

INNER = 8192
WIDTH = 4096
RANK = 32
TOK_DEV = 512
SEQ_DEV = 4
MAXLEN = 256
LAYERS = 4
QUERIES = 8
SEQS = 16
TOKENS = 2048


def packing(key):
    shards = SEQS // SEQ_DEV
    key_weight, key_place = jax.random.split(key)
    weights = jax.random.randint(key_weight, (shards, SEQ_DEV), 1, 64)
    longest = jax.random.randint(key_place, (shards,), 0, SEQ_DEV)
    is_long = jnp.arange(SEQ_DEV)[None, :] == longest[:, None]
    weights = jnp.where(is_long, 0, weights)
    spare = TOK_DEV - MAXLEN - SEQ_DEV
    others = 1 + spare * weights // jnp.sum(weights, axis=1, keepdims=True)
    seq_lengths = jnp.where(is_long, MAXLEN, others).astype(jnp.int32)
    boundary = jnp.cumsum(seq_lengths, axis=1)
    places = jnp.arange(TOK_DEV, dtype=jnp.int32)
    owners = jnp.sum((places[None, None, :] >= boundary[:, :, None]).astype(jnp.int32), axis=1)
    return (seq_lengths.reshape(-1), owners.reshape(-1).astype(jnp.int32))


def draw_lengths(key, part):
    return packing(key)[0]


def draw_segment_ids(key, part):
    return packing(key)[1]


def block_scale(stream_key, shape, cuts, least, top_value):
    loudness, own = 1.0, jax.random.fold_in(stream_key, 6)
    for axis_at, parts in cuts:
        steps = jnp.exp(jax.random.uniform(jax.random.fold_in(own, axis_at), (parts,), jnp.float32, least / len(cuts), top_value / len(cuts)))
        loudness = loudness * jnp.repeat(steps, shape[axis_at] // parts).reshape([-1 if axis == axis_at else 1 for axis in range(len(shape))])
    return loudness


def gaussian(stream_key, extent, width, bound, pieces=(), held_as=jnp.bfloat16):
    gain = block_scale(stream_key, extent, pieces, -0.22, 0.18) if pieces else 1.0
    drawn = jax.random.normal(stream_key, extent, jnp.float32) * width * gain
    return jnp.minimum(jnp.maximum(drawn, -bound), bound).astype(held_as)


def setup_inputs(seed: int = 0, part: int = 0) -> dict:
    streams_of = jax.random.split(jax.random.key(seed), 7)
    part_splits = jax.random.split(jax.random.fold_in(streams_of[6], part), 7)
    activations = gaussian(part_splits[0], (LAYERS, TOKENS, INNER), 1.0, 6.0, ((0, 4), (1, 4)))
    gradients = gaussian(part_splits[1], (LAYERS, TOKENS, WIDTH), 1.0, 6.0, ((0, 4), (1, 4)))
    left_factors = gaussian(part_splits[2], (LAYERS, QUERIES * RANK, INNER), INNER ** -0.5, 0.0625, ((0, 4), (1, 4)))
    right_factors = gaussian(part_splits[3], (LAYERS, QUERIES * RANK, WIDTH), WIDTH ** -0.5, 0.09375, ((0, 4), (1, 4)))
    lengths = draw_lengths(jax.random.fold_in(jax.random.fold_in(streams_of[6], part), 71), part)
    segment_ids = draw_segment_ids(jax.random.fold_in(jax.random.fold_in(streams_of[6], part), 71), part)
    return {"activations": activations, "gradients": gradients, "left_factors": left_factors, "right_factors": right_factors, "lengths": lengths, "segment_ids": segment_ids}


def token_scores(acts_layer, grads_layer, left_layer, right_layer):
    proj_left = lax.dot_general(acts_layer, left_layer, (((1,), (1,)), ((), ())), preferred_element_type=jnp.float32)
    proj_right = lax.dot_general(grads_layer, right_layer, (((1,), (1,)), ((), ())), preferred_element_type=jnp.float32)
    product = proj_left * proj_right
    return jnp.sum(product.reshape(product.shape[0], QUERIES, RANK), axis=-1)


def reference(activations, gradients, left_factors, right_factors, lengths, segment_ids):
    shards = SEQS // SEQ_DEV
    member_mask = (segment_ids.reshape(shards, 1, TOK_DEV) == jnp.arange(SEQ_DEV, dtype=jnp.int32)[None, :, None]).astype(jnp.float32)
    totals = jnp.zeros((shards, SEQ_DEV, QUERIES), jnp.float32)
    for depth in range(LAYERS):
        per_token = token_scores(activations[depth], gradients[depth], left_factors[depth], right_factors[depth])
        per_token = per_token.reshape(shards, TOK_DEV, QUERIES)
        totals = totals + jnp.einsum("sgt,stq->sgq", member_mask, per_token, precision=lax.Precision.HIGHEST)
    return totals.reshape(SEQS, QUERIES) / lengths.astype(jnp.float32)[:, None]
```

```python
import functools

import jax
import jax.numpy as jnp
from jax import lax
from jax.experimental import pallas as pl
from jax.experimental.pallas import tpu as pltpu
from jax.sharding import PartitionSpec as P

RANK = 32
LANES = 128
SUBLANES = 8
CHUNK = 512
WINDOW = 0
MESH = pl.DeviceIdType.MESH


def chunks_of(inner, width, chunk):
    left = [(0, k, chunk) for k in range(0, inner, chunk)]
    right = [(1, k, chunk) for k in range(0, width, chunk)]
    return left + right


def kernel(
    chunks, layers, chips, query_lanes,
    act, grad, left, right, seg,
    out,
    act_v, grad_v, left_v, right_v, seg_v, acc, part, inbox,
    load_sem, near_send, near_recv, cross_send, cross_recv, pass_send, pass_recv,
    sum_send, sum_recv,
):
    rows = left.shape[1]
    dp, layer = lax.axis_index("dp"), lax.axis_index("layer")
    chip, core = lax.div(dp, 2), lax.rem(dp, 2)
    sibling = {"dp": chip * 2 + 1 - core}
    mine = pl.ds(pl.multiple_of(core * rows, rows), rows)
    own, held = (left, right), (left_v, right_v)
    tokens = (act_v, grad_v)

    partners = [{"dp": lax.rem(chip + s, chips) * 2 + core} for s in range(1, chips)]
    origins = [lax.rem(chip + chips - s, chips) for s in range(1, chips)]
    others = [{"layer": lax.rem(layer + d, layers)} for d in range(1, layers)]

    barrier = pltpu.get_barrier_semaphore()
    peers = [sibling] + partners + others
    for peer in peers:
        pl.semaphore_signal(barrier, inc=1, device_id=peer, device_id_type=MESH)

    loads = [
        pltpu.make_async_copy(left.at[0], left_v.at[chip, mine], load_sem.at[0]),
        pltpu.make_async_copy(right.at[0], right_v.at[chip, mine], load_sem.at[1]),
        pltpu.make_async_copy(act.at[0], act_v, load_sem.at[2]),
        pltpu.make_async_copy(grad.at[0], grad_v, load_sem.at[3]),
        pltpu.make_async_copy(seg, seg_v, load_sem.at[4]),
    ]
    for load in loads:
        load.start()
    pl.semaphore_wait(barrier, len(peers))

    def cross_copy(s, i):
        side, k, size = chunks[i]
        return pltpu.make_async_remote_copy(
            src_ref=own[side].at[0, :, pl.ds(k, size)],
            dst_ref=held[side].at[chip, mine, pl.ds(k, size)],
            send_sem=cross_send.at[s, i], recv_sem=cross_recv.at[s, i],
            device_id=partners[s], device_id_type=MESH,
        )

    def pass_copy(s, i):
        side, k, size = chunks[i]
        block = held[side].at[origins[s], mine, pl.ds(k, size)]
        return pltpu.make_async_remote_copy(
            src_ref=block, dst_ref=block,
            send_sem=pass_send.at[s, i], recv_sem=pass_recv.at[s, i],
            device_id=sibling, device_id_type=MESH,
        )

    def near_copy(side):
        return pltpu.make_async_remote_copy(
            src_ref=own[side].at[0], dst_ref=held[side].at[chip, mine],
            send_sem=near_send.at[side], recv_sem=near_recv.at[side],
            device_id=sibling, device_id_type=MESH,
        )

    steps = [(s, i) for s in range(chips - 1) for i in range(len(chunks))]
    crossing = [cross_copy(s, i) for s, i in steps]
    passing = [pass_copy(s, i) for s, i in steps]
    near = [near_copy(0), near_copy(1)]
    ahead = WINDOW if WINDOW and chips == 2 else len(steps)
    for copy in crossing[:ahead]:
        copy.start()
    for copy in near:
        copy.start()

    def project(slot, source, i):
        side, k, size = chunks[i]
        product = lax.dot_general(
            tokens[side][:, k:k + size], held[side][source, :, k:k + size],
            (((1,), (1,)), ((), ())), preferred_element_type=jnp.float32,
        )
        if k:
            product = acc[slot, side] + product
        acc[slot, side] = product

    def reduce_tokens(slot, source):
        token_count = seg_v.shape[1]
        sequence = lax.broadcasted_iota(jnp.int32, (SUBLANES, token_count), 0)
        member = (sequence == seg_v[...]).astype(jnp.float32)
        part[source] = jnp.dot(
            member, acc[slot, 0] * acc[slot, 1],
            precision=lax.Precision.HIGHEST, preferred_element_type=jnp.float32,
        )

    for load in loads:
        load.wait()
    behind = None
    for n, (s, i) in enumerate(steps):
        if n < len(chunks):
            if n == 0 or chunks[n][0] != chunks[n - 1][0]:
                near[chunks[n][0]].wait_recv()
            project(0, chip, n)
            if n == len(chunks) - 1:
                reduce_tokens(0, chip)
        crossing[n].wait_recv()
        passing[n].start()
        if n + ahead < len(steps):
            crossing[n].wait_send()
            crossing[n + ahead].start()
        if behind is not None:
            passing[n - 1].wait_recv()
            project(1, origins[behind[0]], behind[1])
            if behind[1] == len(chunks) - 1:
                reduce_tokens(1, origins[behind[0]])
        behind = (s, i)
    passing[-1].wait_recv()
    project(1, origins[behind[0]], behind[1])
    reduce_tokens(1, origins[behind[0]])

    def sum_copy(d):
        target = lax.rem(layer + d, layers)
        return pltpu.make_async_remote_copy(
            src_ref=part.at[lax.div(target * query_lanes, LANES)], dst_ref=inbox.at[d - 1],
            send_sem=sum_send.at[d - 1], recv_sem=sum_recv.at[d - 1],
            device_id=others[d - 1], device_id_type=MESH,
        )

    summing = [sum_copy(d) for d in range(1, layers)]
    for copy in summing:
        copy.start()
    first = layer * query_lanes
    total = part[lax.div(first, LANES)]
    for n in range(len(steps)):
        if n + ahead >= len(steps):
            crossing[n].wait_send()
        passing[n].wait_send()
    for copy in near:
        copy.wait_send()
    for d in range(layers - 1):
        summing[d].wait_recv()
        total = total + inbox[d]
    query = lax.div(lax.broadcasted_iota(jnp.int32, total.shape, 1), RANK)
    first_query = lax.div(lax.rem(first, LANES), RANK)
    for j in range(query_lanes // RANK):
        score = jnp.sum(jnp.where(query == first_query + j, total, 0.0), axis=1, keepdims=True)
        out[:, j:j + 1] = score[:out.shape[0]]
    for copy in summing:
        copy.wait_send()


def local(mesh, activations, gradients, left_factors, right_factors, lengths, segment_ids):
    layers, chips = mesh.shape["layer"], mesh.shape["dp"] // 2
    rows, inner = left_factors.shape[1:]
    width = right_factors.shape[2]
    token_count, seq_count = segment_ids.shape[0], lengths.shape[0]
    query_lanes = 2 * chips * rows // layers
    chunks = chunks_of(inner, width, CHUNK if chips == 2 else 2048)
    hbm = pl.BlockSpec(memory_space=pl.ANY)
    dma = pltpu.SemaphoreType.DMA
    steps = (chips - 1, len(chunks))
    summed = pl.pallas_call(
        functools.partial(kernel, chunks, layers, chips, query_lanes),
        out_shape=jax.ShapeDtypeStruct((seq_count, query_lanes // RANK), jnp.float32),
        in_specs=[hbm] * 5,
        out_specs=pl.BlockSpec(memory_space=pltpu.VMEM),
        scratch_shapes=[
            pltpu.VMEM((token_count, inner), jnp.bfloat16),
            pltpu.VMEM((token_count, width), jnp.bfloat16),
            pltpu.VMEM((chips, 2 * rows, inner), jnp.bfloat16),
            pltpu.VMEM((chips, 2 * rows, width), jnp.bfloat16),
            pltpu.VMEM((1, token_count), jnp.int32),
            pltpu.VMEM((2, 2, token_count, 2 * rows), jnp.float32),
            pltpu.VMEM((chips, SUBLANES, 2 * rows), jnp.float32),
            pltpu.VMEM((layers - 1, SUBLANES, 2 * rows), jnp.float32),
            dma((5,)), dma((2,)), dma((2,)),
            dma(steps), dma(steps), dma(steps), dma(steps),
            dma((layers - 1,)), dma((layers - 1,)),
        ],
        compiler_params=pltpu.CompilerParams(
            collective_id=0, has_side_effects=True, vmem_limit_bytes=56 * 2**20
        ),
    )(activations, gradients, left_factors, right_factors, segment_ids.reshape(1, -1))
    return summed / lengths.astype(jnp.float32)[:, None]


def solution(mesh):
    return jax.shard_map(
        functools.partial(local, mesh),
        mesh=mesh,
        in_specs=(
            P("layer", ("groups", "dp"), None),
            P("layer", ("groups", "dp"), None),
            P("layer", ("groups", "dp"), None),
            P("layer", ("groups", "dp"), None),
            P(("groups", "dp")),
            P(("groups", "dp")),
        ),
        out_specs=P(("groups", "dp"), "layer"),
        check_vma=False,
    )
```

```python
import functools

import jax
import jax.numpy as jnp
from jax import lax
from jax.experimental import pallas as pl
from jax.experimental.pallas import tpu as pltpu
from jax.sharding import PartitionSpec as P

RANK = 32
LANES = 128
SUBLANES = 8
CHUNK = 1024
TAPER = ()
WINDOW = 0
MESH = pl.DeviceIdType.MESH


def chunks_of(inner, width, chunk, taper):
    left = [(0, k, chunk) for k in range(0, inner, chunk)]
    right = [(1, k, chunk) for k in range(0, width - sum(taper), chunk)]
    last = [(1, width - sum(taper[n:]), size) for n, size in enumerate(taper)]
    return left + right + last


def kernel(
    chunks, layers, chips, query_lanes,
    act, grad, left, right, seg, length,
    out,
    act_v, grad_v, left_v, right_v, seg_v, length_s, acc, part, inbox,
    load_sem, near_send, near_recv, cross_send, cross_recv, pass_send, pass_recv,
    sum_send, sum_recv,
):
    rows = left.shape[1]
    dp, layer = lax.axis_index("dp"), lax.axis_index("layer")
    chip, core = lax.div(dp, 2), lax.rem(dp, 2)
    sibling = {"dp": chip * 2 + 1 - core}
    mine = pl.ds(pl.multiple_of(core * rows, rows), rows)
    own, held = (left, right), (left_v, right_v)
    tokens = (act_v, grad_v)

    partners = [{"dp": lax.rem(chip + s, chips) * 2 + core} for s in range(1, chips)]
    origins = [lax.rem(chip + chips - s, chips) for s in range(1, chips)]
    others = [{"layer": lax.rem(layer + d, layers)} for d in range(1, layers)]

    barrier = pltpu.get_barrier_semaphore()
    peers = others + partners + [sibling]
    for peer in peers:
        pl.semaphore_signal(barrier, inc=1, device_id=peer, device_id_type=MESH)

    loads = [
        pltpu.make_async_copy(left.at[0], left_v.at[chip, mine], load_sem.at[0]),
        pltpu.make_async_copy(right.at[0], right_v.at[chip, mine], load_sem.at[1]),
        pltpu.make_async_copy(act.at[0], act_v, load_sem.at[2]),
        pltpu.make_async_copy(grad.at[0], grad_v, load_sem.at[3]),
        pltpu.make_async_copy(seg, seg_v, load_sem.at[4]),
        pltpu.make_async_copy(length, length_s, load_sem.at[5]),
    ]
    for load in loads:
        load.start()
    pl.semaphore_wait(barrier, len(peers))

    def cross_copy(s, i):
        side, k, size = chunks[i]
        return pltpu.make_async_remote_copy(
            src_ref=own[side].at[0, :, pl.ds(k, size)],
            dst_ref=held[side].at[chip, mine, pl.ds(k, size)],
            send_sem=cross_send.at[s, i], recv_sem=cross_recv.at[s, i],
            device_id=partners[s], device_id_type=MESH,
        )

    def pass_copy(s, i):
        side, k, size = chunks[i]
        block = held[side].at[origins[s], mine, pl.ds(k, size)]
        return pltpu.make_async_remote_copy(
            src_ref=block, dst_ref=block,
            send_sem=pass_send.at[s, i], recv_sem=pass_recv.at[s, i],
            device_id=sibling, device_id_type=MESH,
        )

    def near_copy(side):
        return pltpu.make_async_remote_copy(
            src_ref=own[side].at[0], dst_ref=held[side].at[chip, mine],
            send_sem=near_send.at[side], recv_sem=near_recv.at[side],
            device_id=sibling, device_id_type=MESH,
        )

    steps = [(s, i) for s in range(chips - 1) for i in range(len(chunks))]
    crossing = [cross_copy(s, i) for s, i in steps]
    passing = [pass_copy(s, i) for s, i in steps]
    near = [near_copy(0), near_copy(1)]
    ahead = WINDOW if WINDOW and chips == 2 else len(steps)
    for copy in crossing[:ahead]:
        copy.start()
    for copy in near:
        copy.start()

    def project(slot, source, i):
        side, k, size = chunks[i]
        product = lax.dot_general(
            tokens[side][:, k:k + size], held[side][source, :, k:k + size],
            (((1,), (1,)), ((), ())), preferred_element_type=jnp.float32,
        )
        if k:
            product = acc[slot, side] + product
        acc[slot, side] = product

    def reduce_tokens(slot, source):
        token_count = seg_v.shape[1]
        sequence = lax.broadcasted_iota(jnp.int32, (SUBLANES, token_count), 0)
        member = (sequence == seg_v[...]).astype(jnp.float32)
        part[source] = jnp.dot(
            member, acc[slot, 0] * acc[slot, 1],
            precision=lax.Precision.HIGHEST, preferred_element_type=jnp.float32,
        )

    for load in loads:
        load.wait()
    behind = None
    for n, (s, i) in enumerate(steps):
        if n < len(chunks):
            if n == 0 or chunks[n][0] != chunks[n - 1][0]:
                near[chunks[n][0]].wait_recv()
            project(0, chip, n)
            if n == len(chunks) - 1:
                reduce_tokens(0, chip)
        crossing[n].wait_recv()
        passing[n].start()
        if n + ahead < len(steps):
            crossing[n].wait_send()
            crossing[n + ahead].start()
        if behind is not None:
            passing[n - 1].wait_recv()
            project(1, origins[behind[0]], behind[1])
            if behind[1] == len(chunks) - 1:
                reduce_tokens(1, origins[behind[0]])
        behind = (s, i)
    passing[-1].wait_recv()
    project(1, origins[behind[0]], behind[1])
    reduce_tokens(1, origins[behind[0]])

    def sum_copy(d):
        target = lax.rem(layer + d, layers)
        return pltpu.make_async_remote_copy(
            src_ref=part.at[lax.div(target * query_lanes, LANES)], dst_ref=inbox.at[d - 1],
            send_sem=sum_send.at[d - 1], recv_sem=sum_recv.at[d - 1],
            device_id=others[d - 1], device_id_type=MESH,
        )

    summing = [sum_copy(d) for d in range(1, layers)]
    for copy in summing:
        copy.start()
    row = lax.broadcasted_iota(jnp.int32, part.shape[1:], 0)
    lane = lax.broadcasted_iota(jnp.int32, part.shape[1:], 1)
    count = jnp.ones((1, LANES), jnp.int32)
    for g in range(out.shape[1]):
        count = jnp.where(lane[:1] == g, length_s[g], count)
    count = count.astype(jnp.float32)
    first = layer * query_lanes
    total = part[lax.div(first, LANES)]
    for n in range(len(steps)):
        if n + ahead >= len(steps):
            crossing[n].wait_send()
        passing[n].wait_send()
    for copy in near:
        copy.wait_send()
    for d in range(layers - 1):
        summing[d].wait_recv()
        total = total + inbox[d]
    query = lax.div(lane, RANK)
    first_query = lax.div(lax.rem(first, LANES), RANK)
    for j in range(query_lanes // RANK):
        score = jnp.sum(jnp.where(query == first_query + j, total, 0.0), axis=1, keepdims=True)
        score = jnp.sum(jnp.where(row == lane, score, 0.0), axis=0, keepdims=True)
        out[j:j + 1, :] = (score / count)[:, :out.shape[1]]
    for copy in summing:
        copy.wait_send()


def local(mesh, activations, gradients, left_factors, right_factors, lengths, segment_ids):
    layers, chips = mesh.shape["layer"], mesh.shape["dp"] // 2
    rows, inner = left_factors.shape[1:]
    width = right_factors.shape[2]
    token_count, seq_count = segment_ids.shape[0], lengths.shape[0]
    query_lanes = 2 * chips * rows // layers
    chunks = chunks_of(inner, width, *((CHUNK, TAPER) if chips == 2 else (2048, ())))
    hbm = pl.BlockSpec(memory_space=pl.ANY)
    dma = pltpu.SemaphoreType.DMA
    steps = (chips - 1, len(chunks))
    scores = pl.pallas_call(
        functools.partial(kernel, chunks, layers, chips, query_lanes),
        out_shape=jax.ShapeDtypeStruct((query_lanes // RANK, seq_count), jnp.float32),
        in_specs=[hbm] * 6,
        out_specs=pl.BlockSpec(memory_space=pltpu.VMEM),
        scratch_shapes=[
            pltpu.VMEM((token_count, inner), jnp.bfloat16),
            pltpu.VMEM((token_count, width), jnp.bfloat16),
            pltpu.VMEM((chips, 2 * rows, inner), jnp.bfloat16),
            pltpu.VMEM((chips, 2 * rows, width), jnp.bfloat16),
            pltpu.VMEM((1, token_count), jnp.int32),
            pltpu.SMEM((seq_count,), jnp.int32),
            pltpu.VMEM((2, 2, token_count, 2 * rows), jnp.float32),
            pltpu.VMEM((chips, SUBLANES, 2 * rows), jnp.float32),
            pltpu.VMEM((layers - 1, SUBLANES, 2 * rows), jnp.float32),
            dma((6,)), dma((2,)), dma((2,)),
            dma(steps), dma(steps), dma(steps), dma(steps),
            dma((layers - 1,)), dma((layers - 1,)),
        ],
        compiler_params=pltpu.CompilerParams(
            collective_id=0, has_side_effects=True, vmem_limit_bytes=56 * 2**20
        ),
    )(activations, gradients, left_factors, right_factors, segment_ids.reshape(1, -1), lengths)
    return scores.T


def solution(mesh):
    return jax.shard_map(
        functools.partial(local, mesh),
        mesh=mesh,
        in_specs=(
            P("layer", ("groups", "dp"), None),
            P("layer", ("groups", "dp"), None),
            P("layer", ("groups", "dp"), None),
            P("layer", ("groups", "dp"), None),
            P(("groups", "dp")),
            P(("groups", "dp")),
        ),
        out_specs=P(("groups", "dp"), "layer"),
        check_vma=False,
    )
```

```python
import functools

import jax
import jax.numpy as jnp
from jax import lax
from jax.experimental import pallas as pl
from jax.experimental.pallas import tpu as pltpu
from jax.sharding import PartitionSpec as P

RANK = 32
LANES = 128
SUBLANES = 8
CHUNK = 1024
TAPER = ()
WINDOW = 0
MESH = pl.DeviceIdType.MESH


def chunks_of(inner, width, chunk, taper):
    left = [(0, k, chunk) for k in range(0, inner, chunk)]
    right = [(1, k, chunk) for k in range(0, width - sum(taper), chunk)]
    last = [(1, width - sum(taper[n:]), size) for n, size in enumerate(taper)]
    return left + right + last


def kernel(
    chunks, layers, chips, query_lanes,
    act, grad, left, right, seg, length,
    out,
    act_v, grad_v, left_v, right_v, seg_v, length_s, acc, part, inbox,
    load_sem, near_send, near_recv, cross_send, cross_recv, pass_send, pass_recv,
    sum_send, sum_recv,
):
    rows = left.shape[1]
    dp, layer = lax.axis_index("dp"), lax.axis_index("layer")
    chip, core = lax.div(dp, 2), lax.rem(dp, 2)
    sibling = {"dp": chip * 2 + 1 - core}
    mine = pl.ds(pl.multiple_of(core * rows, rows), rows)
    own, held = (left, right), (left_v, right_v)
    tokens = (act_v, grad_v)

    partners = [{"dp": lax.rem(chip + s, chips) * 2 + core} for s in range(1, chips)]
    origins = [lax.rem(chip + chips - s, chips) for s in range(1, chips)]
    others = [{"layer": lax.rem(layer + d, layers)} for d in range(1, layers)]

    barrier = pltpu.get_barrier_semaphore()
    peers = others + partners + [sibling]
    for peer in peers:
        pl.semaphore_signal(barrier, inc=1, device_id=peer, device_id_type=MESH)

    loads = [
        pltpu.make_async_copy(left.at[0], left_v.at[chip, mine], load_sem.at[0]),
        pltpu.make_async_copy(right.at[0], right_v.at[chip, mine], load_sem.at[1]),
        pltpu.make_async_copy(act.at[0], act_v, load_sem.at[2]),
        pltpu.make_async_copy(grad.at[0], grad_v, load_sem.at[3]),
        pltpu.make_async_copy(seg, seg_v, load_sem.at[4]),
        pltpu.make_async_copy(length, length_s, load_sem.at[5]),
    ]
    for load in loads:
        load.start()
    pl.semaphore_wait(barrier, len(peers))

    def cross_copy(s, i):
        side, k, size = chunks[i]
        return pltpu.make_async_remote_copy(
            src_ref=own[side].at[0, :, pl.ds(k, size)],
            dst_ref=held[side].at[chip, mine, pl.ds(k, size)],
            send_sem=cross_send.at[s, i], recv_sem=cross_recv.at[s, i],
            device_id=partners[s], device_id_type=MESH,
        )

    def pass_copy(s, i):
        side, k, size = chunks[i]
        block = held[side].at[origins[s], mine, pl.ds(k, size)]
        return pltpu.make_async_remote_copy(
            src_ref=block, dst_ref=block,
            send_sem=pass_send.at[s, i], recv_sem=pass_recv.at[s, i],
            device_id=sibling, device_id_type=MESH,
        )

    def near_copy(side):
        return pltpu.make_async_remote_copy(
            src_ref=own[side].at[0], dst_ref=held[side].at[chip, mine],
            send_sem=near_send.at[side], recv_sem=near_recv.at[side],
            device_id=sibling, device_id_type=MESH,
        )

    steps = [(s, i) for s in range(chips - 1) for i in range(len(chunks))]
    crossing = [cross_copy(s, i) for s, i in steps]
    passing = [pass_copy(s, i) for s, i in steps]
    near = [near_copy(0), near_copy(1)]
    ahead = WINDOW if WINDOW and chips == 2 else len(steps)
    for copy in crossing[:ahead]:
        copy.start()
    for copy in near:
        copy.start()

    def project(slot, source, i):
        side, k, size = chunks[i]
        product = lax.dot_general(
            tokens[side][:, k:k + size], held[side][source, :, k:k + size],
            (((1,), (1,)), ((), ())), preferred_element_type=jnp.float32,
        )
        if k:
            product = acc[slot, side] + product
        acc[slot, side] = product

    def reduce_tokens(slot, source):
        token_count = seg_v.shape[1]
        sequence = lax.broadcasted_iota(jnp.int32, (SUBLANES, token_count), 0)
        member = (sequence == seg_v[...]).astype(jnp.bfloat16)
        rest, total = acc[slot, 0] * acc[slot, 1], 0.0
        for _ in range(3):
            piece = rest.astype(jnp.bfloat16)
            rest = rest - piece.astype(jnp.float32)
            total += jnp.dot(member, piece, preferred_element_type=jnp.float32)
        part[source] = total

    for load in loads:
        load.wait()
    behind = None
    for n, (s, i) in enumerate(steps):
        if n < len(chunks):
            if n == 0 or chunks[n][0] != chunks[n - 1][0]:
                near[chunks[n][0]].wait_recv()
            project(0, chip, n)
            if n == len(chunks) - 1:
                reduce_tokens(0, chip)
        crossing[n].wait_recv()
        passing[n].start()
        if n + ahead < len(steps):
            crossing[n].wait_send()
            crossing[n + ahead].start()
        if behind is not None:
            passing[n - 1].wait_recv()
            project(1, origins[behind[0]], behind[1])
            if behind[1] == len(chunks) - 1:
                reduce_tokens(1, origins[behind[0]])
        behind = (s, i)
    passing[-1].wait_recv()
    project(1, origins[behind[0]], behind[1])
    reduce_tokens(1, origins[behind[0]])

    def sum_copy(d):
        target = lax.rem(layer + d, layers)
        return pltpu.make_async_remote_copy(
            src_ref=part.at[lax.div(target * query_lanes, LANES)], dst_ref=inbox.at[d - 1],
            send_sem=sum_send.at[d - 1], recv_sem=sum_recv.at[d - 1],
            device_id=others[d - 1], device_id_type=MESH,
        )

    summing = [sum_copy(d) for d in range(1, layers)]
    for copy in summing:
        copy.start()
    row = lax.broadcasted_iota(jnp.int32, part.shape[1:], 0)
    lane = lax.broadcasted_iota(jnp.int32, part.shape[1:], 1)
    count = jnp.ones((1, LANES), jnp.int32)
    for g in range(out.shape[1]):
        count = jnp.where(lane[:1] == g, length_s[g], count)
    count = count.astype(jnp.float32)
    first = layer * query_lanes
    total = part[lax.div(first, LANES)]
    for n in range(len(steps)):
        if n + ahead >= len(steps):
            crossing[n].wait_send()
        passing[n].wait_send()
    for copy in near:
        copy.wait_send()
    for d in range(layers - 1):
        summing[d].wait_recv()
        total = total + inbox[d]
    query = lax.div(lane, RANK)
    first_query = lax.div(lax.rem(first, LANES), RANK)
    for j in range(query_lanes // RANK):
        score = jnp.sum(jnp.where(query == first_query + j, total, 0.0), axis=1, keepdims=True)
        score = jnp.sum(jnp.where(row == lane, score, 0.0), axis=0, keepdims=True)
        out[j:j + 1, :] = (score / count)[:, :out.shape[1]]
    for copy in summing:
        copy.wait_send()


def local(mesh, activations, gradients, left_factors, right_factors, lengths, segment_ids):
    layers, chips = mesh.shape["layer"], mesh.shape["dp"] // 2
    rows, inner = left_factors.shape[1:]
    width = right_factors.shape[2]
    token_count, seq_count = segment_ids.shape[0], lengths.shape[0]
    query_lanes = 2 * chips * rows // layers
    chunks = chunks_of(inner, width, *((CHUNK, TAPER) if chips == 2 else (2048, ())))
    hbm = pl.BlockSpec(memory_space=pl.ANY)
    dma = pltpu.SemaphoreType.DMA
    steps = (chips - 1, len(chunks))
    scores = pl.pallas_call(
        functools.partial(kernel, chunks, layers, chips, query_lanes),
        out_shape=jax.ShapeDtypeStruct((query_lanes // RANK, seq_count), jnp.float32),
        in_specs=[hbm] * 6,
        out_specs=pl.BlockSpec(memory_space=pltpu.VMEM),
        scratch_shapes=[
            pltpu.VMEM((token_count, inner), jnp.bfloat16),
            pltpu.VMEM((token_count, width), jnp.bfloat16),
            pltpu.VMEM((chips, 2 * rows, inner), jnp.bfloat16),
            pltpu.VMEM((chips, 2 * rows, width), jnp.bfloat16),
            pltpu.VMEM((1, token_count), jnp.int32),
            pltpu.SMEM((seq_count,), jnp.int32),
            pltpu.VMEM((2, 2, token_count, 2 * rows), jnp.float32),
            pltpu.VMEM((chips, SUBLANES, 2 * rows), jnp.float32),
            pltpu.VMEM((layers - 1, SUBLANES, 2 * rows), jnp.float32),
            dma((6,)), dma((2,)), dma((2,)),
            dma(steps), dma(steps), dma(steps), dma(steps),
            dma((layers - 1,)), dma((layers - 1,)),
        ],
        compiler_params=pltpu.CompilerParams(
            collective_id=0, has_side_effects=True, vmem_limit_bytes=56 * 2**20
        ),
    )(activations, gradients, left_factors, right_factors, segment_ids.reshape(1, -1), lengths)
    return scores.T


def solution(mesh):
    return jax.shard_map(
        functools.partial(local, mesh),
        mesh=mesh,
        in_specs=(
            P("layer", ("groups", "dp"), None),
            P("layer", ("groups", "dp"), None),
            P("layer", ("groups", "dp"), None),
            P("layer", ("groups", "dp"), None),
            P(("groups", "dp")),
            P(("groups", "dp")),
        ),
        out_specs=P(("groups", "dp"), "layer"),
        check_vma=False,
    )
```
